32 devices in a mesh: parts: 2 (over y), row: 4 (over z), col: 4 (over x, core).
Axes of the slice: x: 2, y: 2, z: 4, core: 2. Of those that a mesh axis runs over, the one named last changes fastest.
Arguments:
- pair_acts: float32 [256, 128, 128], P(('parts', 'row'), 'col'), parts along dimension 0, may hold values from -6 to 6
- residue_mask: int32 [256], P('parts'), parts along dimension 0, may hold values 0 or 1
- norm_gain: float32 [128], replicated, may hold values from 0.1 to 1.9
- norm_bias: float32 [128], replicated, may hold values from -3 to 3
- w_left: bfloat16 [128, 256], replicated, may hold values from -0.5 to 0.5
- w_right: bfloat16 [128, 256], replicated, may hold values from -0.5 to 0.5
- w_gate: bfloat16 [128, 128], replicated, may hold values from -0.5 to 0.5
- out_gain: float32 [128], replicated, may hold values from 0.1 to 1.9
- out_bias: float32 [128], replicated, may hold values from -3 to 3
- w_out: bfloat16 [128, 128], replicated, may hold values from -0.5 to 0.5
Outputs:
- update: float32 [256, 128, 128], P(('parts', 'row'), 'col'), parts along dimension 0
The draws below stay inside these ranges and needn't reach their ends.
There are 2 independent parts, one for each index of `parts`. The reference program is written for one: setup_inputs(seed, part) draws one part's arguments, and reference() takes and returns one part's arrays. A program takes and returns all parts, laid end to end along the dimension named above; an argument that names none is the same for every part. Nothing has to cross between parts.
All inputs are finite; a program needn't handle non-finite values.
Results may differ from the reference program's by a relative error of at most 0.0042.
Values may be sent and summed in bfloat16 or wider, within the bound.
A program may use at most 128 MiB of HBM per device.

```python
import jax
import jax.numpy as jnp
from jax import lax

C = 128
H = 128
N = 128


def place_ends(result, stream_key, smallest, largest):
    spot = [jax.random.randint(jax.random.fold_in(stream_key, axis), (), 0, length) for axis, length in enumerate(result.shape)]
    longest = result.shape.index(max(result.shape))
    beside = spot[:longest] + [(spot[longest] + 1) % result.shape[longest]] + spot[longest + 1:]
    return result.at[tuple(spot)].set(smallest).at[tuple(beside)].set(largest)


def block_scale(stream_key, dims, cuts, least, largest):
    loudness = 1.0
    for axis_at, shards_of in cuts:
        steps = jax.random.uniform(jax.random.fold_in(jax.random.fold_in(stream_key, 6), axis_at), (shards_of,), jnp.float32, least / len(cuts), largest / len(cuts))
        loudness = loudness * jnp.repeat(jnp.exp(steps), dims[axis_at] // shards_of).reshape((-1,) + (1,) * (len(dims) - 1 - axis_at))
    return loudness


def gaussian(key, dims, spread, limit, pieces=(), kind=jnp.bfloat16):
    result = jax.random.normal(key, dims, jnp.float32) * spread
    if len(pieces) > 0:
        result = block_scale(key, dims, pieces, -0.22, 0.18) * result
    return jnp.clip(result, min=-limit, max=limit).astype(kind)


def setup_inputs(seed: int = 0, part: int = 0) -> dict:
    seeds = jax.random.split(jax.random.key(seed), 11)
    own_keys = jax.random.split(jax.random.fold_in(seeds[10], part), 11)
    return {
        "pair_acts": gaussian(own_keys[0], (N, N, C), 1.0, 6.0, ((0, 4), (1, 4)), jnp.float32),
        "residue_mask": place_ends((jax.random.randint(own_keys[1], (N,), 0, 8) < 7).astype(jnp.int32), jax.random.fold_in(own_keys[1], 1), 0, 1),
        "norm_gain": jnp.clip(1.0 + 0.18 * jax.random.normal(seeds[2], (C,), jnp.float32), 0.1, 1.9),
        "norm_bias": gaussian(seeds[3], (C,), 0.5, 3.0, (), jnp.float32),
        "w_left": gaussian(seeds[4], (C, 2 * H), C ** -0.5, 0.5),
        "w_right": gaussian(seeds[5], (C, 2 * H), C ** -0.5, 0.5),
        "w_gate": gaussian(seeds[6], (C, C), C ** -0.5, 0.5),
        "out_gain": jnp.clip(1.0 + 0.18 * jax.random.normal(seeds[7], (H,), jnp.float32), 0.1, 1.9),
        "out_bias": gaussian(seeds[8], (H,), 0.5, 3.0, (), jnp.float32),
        "w_out": gaussian(seeds[9], (H, C), H ** -0.5, 0.5),
    }


def layer_norm(values, gain, bias):
    mean = lax.optimization_barrier(jnp.mean(values, axis=-1, keepdims=True))
    centred = values - mean
    var = lax.optimization_barrier(jnp.mean(centred * centred, axis=-1, keepdims=True))
    return centred * lax.rsqrt(var + 1e-05) * gain + bias

def reference(pair_acts, residue_mask, norm_gain, norm_bias, w_left, w_right, w_gate, out_gain, out_bias, w_out):
    normed = layer_norm(pair_acts, norm_gain, norm_bias).astype(jnp.bfloat16)
    valid = residue_mask.astype(jnp.float32)
    pair_mask = (valid[:, None] * valid[None, :])[..., None]
    normed32 = normed.astype(jnp.float32)
    left = jnp.einsum('ijc,cd->ijd', normed32, w_left.astype(jnp.float32))
    left_act = (jax.nn.sigmoid(left[..., H:]) * left[..., :H] * pair_mask).astype(jnp.bfloat16)
    right = jnp.einsum('ijc,cd->ijd', normed32, w_right.astype(jnp.float32))
    right_act = (jax.nn.sigmoid(right[..., H:]) * right[..., :H] * pair_mask).astype(jnp.bfloat16)
    triangle = jnp.einsum('ikh,jkh->ijh', left_act.astype(jnp.float32), right_act.astype(jnp.float32))
    tri_norm = layer_norm(triangle, out_gain, out_bias).astype(jnp.bfloat16)
    gate = jax.nn.sigmoid(jnp.einsum('ijc,cd->ijd', normed32, w_gate.astype(jnp.float32)))
    projected = jnp.einsum('ijh,hc->ijc', tri_norm.astype(jnp.float32), w_out.astype(jnp.float32))
    return gate * projected
```

```python
import functools

import jax
import jax.numpy as jnp
from jax import lax
from jax.experimental import pallas as pl
from jax.experimental.pallas import tpu as pltpu
from jax.sharding import PartitionSpec as P

F32 = jnp.float32
BF16 = jnp.bfloat16
PIECES = 4
GROUP = 8


def layer_norm(values, gain, bias):
    mean = jnp.mean(values, axis=-1, keepdims=True)
    centred = values - mean
    var = jnp.mean(centred * centred, axis=-1, keepdims=True)
    return centred * lax.rsqrt(var + 1e-05) * gain + bias


def sigmoid(values):
    return 0.5 * jnp.tanh(0.5 * values) + 0.5


def kernel(
    rows,
    cols,
    mask_ref,
    x_ref,
    gain_ref,
    bias_ref,
    w_left_ref,
    w_right_ref,
    w_gate_ref,
    out_gain_ref,
    out_bias_ref,
    w_out_ref,
    out_ref,
    chain,
    right,
    left,
    left32,
    tri,
    gate,
    row_valid,
    up_send,
    up_recv,
    down_send,
    down_recv,
    swap_send,
    swap_recv,
    far_send,
    pair_send,
    left_recv,
):
    z = lax.axis_index("row")
    c = lax.axis_index("col")
    x, core = c // 2, c % 2
    twin = 2 * x + 1 - core
    chips = cols // 2
    ratio = rows // cols
    k_count, i_count, hidden = chain.shape[1:]
    piece = k_count // PIECES
    j_count = ratio * i_count

    barrier = pltpu.get_barrier_semaphore()

    @pl.when(z > 0)
    def _():
        pl.semaphore_signal(barrier, inc=1, device_id={"row": z - 1}, device_id_type=pl.DeviceIdType.MESH)

    @pl.when(z < rows - 1)
    def _():
        pl.semaphore_signal(barrier, inc=1, device_id={"row": z + 1}, device_id_type=pl.DeviceIdType.MESH)

    for step in range(1, cols):
        pl.semaphore_signal(
            barrier, inc=1, device_id={"col": lax.rem(c + step, cols)}, device_id_type=pl.DeviceIdType.MESH
        )

    def part(p):
        return pl.ds(p * piece, piece)

    def up(step, p, block):
        ref = chain.at[block, part(p)]
        return pltpu.make_async_remote_copy(
            ref, ref, up_send.at[step, p], up_recv.at[step, p], {"row": z + 1}, pl.DeviceIdType.MESH
        )

    def down(step, p, block):
        ref = chain.at[block, part(p)]
        return pltpu.make_async_remote_copy(
            ref, ref, down_send.at[step, p], down_recv.at[step, p], {"row": z - 1}, pl.DeviceIdType.MESH
        )

    def swap(p, block):
        return pltpu.make_async_remote_copy(
            chain.at[block, part(p)],
            right.at[c, block % ratio, part(p)],
            swap_send.at[block, p],
            swap_recv.at[c, block % ratio, p],
            {"col": block // ratio},
            pl.DeviceIdType.MESH,
        )

    def keep(p, block):
        return pltpu.make_async_copy(
            chain.at[block, part(p)], right.at[c, block % ratio, part(p)], swap_recv.at[c, block % ratio, p]
        )

    def deliver(p, block):
        @pl.when(block // ratio != c)
        def _():
            swap(p, block).start()

        @pl.when(block // ratio == c)
        def _():
            keep(p, block).start()

    def left_copy(p, owner, target, send):
        ref = left.at[owner, part(p)]
        return pltpu.make_async_remote_copy(
            ref, ref, send, left_recv.at[owner, p], {"col": target}, pl.DeviceIdType.MESH
        )

    def far(p, step):
        return left_copy(p, c, 2 * lax.rem(x + step, chips) + core, far_send.at[step - 1, p])

    def pair(p, step):
        return left_copy(p, 2 * lax.rem(x + step, chips) + core, twin, pair_send.at[step, p])

    for i in range(i_count):
        row_valid[pl.ds(i, 1), :] = jnp.full((1, hidden), mask_ref[z * i_count + i].astype(F32))

    def side(normed, weight, mask):
        both = jnp.dot(normed, weight, preferred_element_type=F32)
        act = sigmoid(both[:, hidden:]) * both[:, :hidden] * mask
        return act.astype(BF16).reshape(piece, i_count, hidden)

    gain, bias = gain_ref[...], bias_ref[...]
    for p in range(PIECES):
        values = jnp.concatenate(
            [x_ref[pl.ds(p * piece + k, i_count, stride=k_count), :] for k in range(piece)], axis=0
        )
        mask = jnp.concatenate(
            [row_valid[...] * mask_ref[c * k_count + p * piece + k].astype(F32) for k in range(piece)], axis=0
        )
        normed = layer_norm(values, gain, bias).astype(BF16)
        chain[z, part(p)] = side(normed, w_right_ref[...], mask)
        if p == 0:
            neighbours = cols - 1 + (z > 0).astype(jnp.int32) + (z < rows - 1).astype(jnp.int32)
            pl.semaphore_wait(barrier, neighbours)

        @pl.when(z < rows - 1)
        def _():
            up(0, p, z).start()

        @pl.when(z > 0)
        def _():
            down(0, p, z).start()

        left[c, part(p)] = side(normed, w_left_ref[...], mask)
        for step in range(1, chips):
            far(p, step).start()
        pair(p, 0).start()
        deliver(p, z)

    tri[...] = jnp.zeros_like(tri)
    flat = GROUP * k_count

    def make_gate(g, carry):
        span = pl.ds(pl.multiple_of(g * flat, flat), flat)
        normed = layer_norm(x_ref[span, :], gain, bias).astype(BF16)
        gate[span, :] = sigmoid(jnp.dot(normed, w_gate_ref[...], preferred_element_type=F32))
        return carry

    lax.fori_loop(0, i_count // GROUP, make_gate, 0)

    def relay(step, p):
        @pl.when(z - 1 - step >= 0)
        def _():
            up(step, p, z - 1 - step).wait_recv()
            if step < rows - 2:

                @pl.when(z < rows - 1)
                def _():
                    up(step + 1, p, z - 1 - step).start()

            deliver(p, z - 1 - step)

        @pl.when(z + 1 + step < rows)
        def _():
            down(step, p, z + 1 + step).wait_recv()
            if step < rows - 2:

                @pl.when(z > 0)
                def _():
                    down(step + 1, p, z + 1 + step).start()

            deliver(p, z + 1 + step)

        if step == 0:
            for other in range(1, chips):
                pair(p, other).wait_recv()
                pair(p, other).start()

    def multiply(p):
        for owner in range(cols):
            for offset in range(ratio):
                ref = right.at[owner, offset, part(p)]
                pltpu.make_async_copy(ref, ref, swap_recv.at[owner, offset, p]).wait()
        for other in range(chips):
            owner = 2 * lax.rem(x + other, chips) + 1 - core
            left_copy(p, owner, twin, pair_send.at[other, p]).wait_recv()

        def widen(owner, carry):
            left32[pl.ds(owner * piece, piece)] = left[owner, part(p)].astype(F32)
            return carry

        lax.fori_loop(0, cols, widen, 0)
        groups = i_count // GROUP

        def block(at, carry):
            offset, first = at // groups, pl.multiple_of((at % groups) * GROUP, GROUP)
            js = pl.ds(pl.multiple_of(offset * i_count, i_count), i_count)

            def add(owner, sums):
                for k in range(piece):
                    other = right[owner, offset, p * piece + k].astype(F32)
                    sums = tuple(
                        total + left32[owner * piece + k, pl.ds(first + g, 1), :] * other
                        for g, total in enumerate(sums)
                    )
                return sums

            sums = tuple(tri[first + g, js, :] for g in range(GROUP))
            sums = lax.fori_loop(0, cols, add, sums)
            for g in range(GROUP):
                tri[first + g, js, :] = sums[g]
            return carry

        lax.fori_loop(0, groups * ratio, block, 0)

    for step in range(rows - 2):
        for p in range(PIECES):
            relay(step, p)
    for p in range(PIECES):
        relay(rows - 2, p)
        if p > 0:
            multiply(p - 1)
    multiply(PIECES - 1)

    def finish(g, carry):
        span = pl.ds(pl.multiple_of(g * flat, flat), flat)
        values = tri[pl.ds(g * GROUP, GROUP)].reshape(flat, hidden)
        normed = layer_norm(values, out_gain_ref[...], out_bias_ref[...]).astype(BF16)
        out_ref[span, :] = gate[span, :] * jnp.dot(normed, w_out_ref[...], preferred_element_type=F32)
        return carry

    lax.fori_loop(0, i_count // GROUP, finish, 0)

    for p in range(PIECES):
        for step in range(rows - 1):

            @pl.when((z < rows - 1) & (z - step >= 0))
            def _():
                up(step, p, z - step).wait_send()

            @pl.when((z > 0) & (z + step < rows))
            def _():
                down(step, p, z + step).wait_send()

        for step in range(1, chips):
            far(p, step).wait_send()
        for step in range(chips):
            pair(p, step).wait_send()
        for block in range(rows):

            @pl.when(block // ratio != c)
            def _():
                swap(p, block).wait_send()


def solution(mesh):
    rows, cols = mesh.shape["row"], mesh.shape["col"]

    def body(pair_acts, residue_mask, norm_gain, norm_bias, w_left, w_right, w_gate, out_gain, out_bias, w_out):
        i_count, k_count, channels = pair_acts.shape
        hidden = w_out.shape[0]
        ratio = rows // cols
        piece = k_count // PIECES
        dma = pltpu.SemaphoreType.DMA
        vmem = pl.BlockSpec(memory_space=pltpu.VMEM)
        flat = pl.pallas_call(
            functools.partial(kernel, rows, cols),
            out_shape=jax.ShapeDtypeStruct((i_count * k_count, channels), F32),
            in_specs=[pl.BlockSpec(memory_space=pltpu.SMEM)] + [vmem] * 9,
            out_specs=vmem,
            scratch_shapes=[
                pltpu.VMEM((rows, k_count, i_count, hidden), BF16),
                pltpu.VMEM((cols, ratio, k_count, i_count, hidden), BF16),
                pltpu.VMEM((cols, k_count, i_count, hidden), BF16),
                pltpu.VMEM((cols * piece, i_count, hidden), F32),
                pltpu.VMEM((i_count, k_count, hidden), F32),
                pltpu.VMEM((i_count * k_count, channels), F32),
                pltpu.VMEM((i_count, hidden), F32),
                dma((rows - 1, PIECES)),
                dma((rows - 1, PIECES)),
                dma((rows - 1, PIECES)),
                dma((rows - 1, PIECES)),
                dma((rows, PIECES)),
                dma((cols, ratio, PIECES)),
                dma((cols // 2 - 1, PIECES)),
                dma((cols // 2, PIECES)),
                dma((cols, PIECES)),
            ],
            compiler_params=pltpu.CompilerParams(
                collective_id=0, has_side_effects=True, vmem_limit_bytes=48 * 1024 * 1024
            ),
        )(
            residue_mask,
            pair_acts.reshape(i_count * k_count, channels),
            norm_gain.reshape(1, channels),
            norm_bias.reshape(1, channels),
            w_left,
            w_right,
            w_gate,
            out_gain.reshape(1, hidden),
            out_bias.reshape(1, hidden),
            w_out,
        )
        return flat.reshape(i_count, k_count, channels)

    placed = (P(("parts", "row"), "col", None), P("parts"), P(), P(), P(), P(), P(), P(), P(), P())
    return jax.shard_map(
        body,
        mesh=mesh,
        in_specs=placed,
        out_specs=P(("parts", "row"), "col", None),
        check_vma=False,
    )
```

```python
import functools

import jax
import jax.numpy as jnp
from jax import lax
from jax.experimental import pallas as pl
from jax.experimental.pallas import tpu as pltpu
from jax.sharding import PartitionSpec as P

F32 = jnp.float32
BF16 = jnp.bfloat16
PIECES = 4
GROUP = 8


def layer_norm(values, gain, bias):
    mean = jnp.mean(values, axis=-1, keepdims=True)
    centred = values - mean
    var = jnp.mean(centred * centred, axis=-1, keepdims=True)
    return centred * lax.rsqrt(var + 1e-05) * gain + bias


def sigmoid(values):
    return 0.5 * jnp.tanh(0.5 * values) + 0.5


def kernel(
    rows,
    cols,
    *refs,
):
    sources, out_ref, held = refs[:10], refs[10], refs[11:21]
    (
        mask_ref,
        x_ref,
        gain_ref,
        bias_ref,
        w_left_ref,
        w_right_ref,
        w_gate_ref,
        out_gain_ref,
        out_bias_ref,
        w_out_ref,
    ) = held
    (
        chain,
        right,
        left,
        left32,
        tri,
        gate,
        row_valid,
        up_send,
        up_recv,
        down_send,
        down_recv,
        swap_send,
        swap_recv,
        far_send,
        pair_send,
        left_recv,
        load_sem,
    ) = refs[21:]
    loads = [
        pltpu.make_async_copy(source, target, load_sem.at[at])
        for at, (source, target) in enumerate(zip(sources, held))
    ]
    for at in (1, 0, 5, 2, 3, 4, 6, 7, 8, 9):
        loads[at].start()
    z = lax.axis_index("row")
    c = lax.axis_index("col")
    x, core = c // 2, c % 2
    twin = 2 * x + 1 - core
    chips = cols // 2
    ratio = rows // cols
    k_count, i_count, hidden = chain.shape[1:]
    piece = k_count // PIECES
    j_count = ratio * i_count

    barrier = pltpu.get_barrier_semaphore()

    @pl.when(z > 0)
    def _():
        pl.semaphore_signal(barrier, inc=1, device_id={"row": z - 1}, device_id_type=pl.DeviceIdType.MESH)

    @pl.when(z < rows - 1)
    def _():
        pl.semaphore_signal(barrier, inc=1, device_id={"row": z + 1}, device_id_type=pl.DeviceIdType.MESH)

    for step in range(1, cols):
        pl.semaphore_signal(
            barrier, inc=1, device_id={"col": lax.rem(c + step, cols)}, device_id_type=pl.DeviceIdType.MESH
        )

    def part(p):
        return pl.ds(p * piece, piece)

    def up(step, p, block):
        ref = chain.at[block, part(p)]
        return pltpu.make_async_remote_copy(
            ref, ref, up_send.at[step, p], up_recv.at[step, p], {"row": z + 1}, pl.DeviceIdType.MESH
        )

    def down(step, p, block):
        ref = chain.at[block, part(p)]
        return pltpu.make_async_remote_copy(
            ref, ref, down_send.at[step, p], down_recv.at[step, p], {"row": z - 1}, pl.DeviceIdType.MESH
        )

    def swap(p, block):
        return pltpu.make_async_remote_copy(
            chain.at[block, part(p)],
            right.at[c, block % ratio, part(p)],
            swap_send.at[block, p],
            swap_recv.at[c, block % ratio, p],
            {"col": block // ratio},
            pl.DeviceIdType.MESH,
        )

    def keep(p, block):
        return pltpu.make_async_copy(
            chain.at[block, part(p)], right.at[c, block % ratio, part(p)], swap_recv.at[c, block % ratio, p]
        )

    def deliver(p, block):
        @pl.when(block // ratio != c)
        def _():
            swap(p, block).start()

        @pl.when(block // ratio == c)
        def _():
            keep(p, block).start()

    def left_copy(p, owner, target, send):
        ref = left.at[owner, part(p)]
        return pltpu.make_async_remote_copy(
            ref, ref, send, left_recv.at[owner, p], {"col": target}, pl.DeviceIdType.MESH
        )

    def far(p, step):
        return left_copy(p, c, 2 * lax.rem(x + step, chips) + core, far_send.at[step - 1, p])

    def pair(p, step):
        return left_copy(p, 2 * lax.rem(x + step, chips) + core, twin, pair_send.at[step, p])

    loads[0].wait()
    for i in range(i_count):
        row_valid[pl.ds(i, 1), :] = jnp.full((1, hidden), mask_ref[z * i_count + i].astype(F32))

    def side(normed, weight, mask):
        both = jnp.dot(normed, weight, preferred_element_type=F32)
        act = sigmoid(both[:, hidden:]) * both[:, :hidden] * mask
        return act.astype(BF16).reshape(piece, i_count, hidden)

    for at in (2, 3, 1, 5, 4):
        loads[at].wait()
    gain, bias = gain_ref[...], bias_ref[...]
    for p in range(PIECES):
        values = jnp.concatenate(
            [x_ref[pl.ds(p * piece + k, i_count, stride=k_count), :] for k in range(piece)], axis=0
        )
        mask = jnp.concatenate(
            [row_valid[...] * mask_ref[c * k_count + p * piece + k].astype(F32) for k in range(piece)], axis=0
        )
        normed = layer_norm(values, gain, bias).astype(BF16)
        chain[z, part(p)] = side(normed, w_right_ref[...], mask)
        if p == 0:
            neighbours = cols - 1 + (z > 0).astype(jnp.int32) + (z < rows - 1).astype(jnp.int32)
            pl.semaphore_wait(barrier, neighbours)

        @pl.when(z < rows - 1)
        def _():
            up(0, p, z).start()

        @pl.when(z > 0)
        def _():
            down(0, p, z).start()

        left[c, part(p)] = side(normed, w_left_ref[...], mask)
        for step in range(1, chips):
            far(p, step).start()
        pair(p, 0).start()
        deliver(p, z)

    tri[...] = jnp.zeros_like(tri)
    for at in (6, 7, 8, 9):
        loads[at].wait()
    flat = GROUP * k_count

    def make_gate(g, carry):
        span = pl.ds(pl.multiple_of(g * flat, flat), flat)
        normed = layer_norm(x_ref[span, :], gain, bias).astype(BF16)
        gate[span, :] = sigmoid(jnp.dot(normed, w_gate_ref[...], preferred_element_type=F32))
        return carry

    lax.fori_loop(0, i_count // GROUP, make_gate, 0)

    def relay(step, p):
        @pl.when(z - 1 - step >= 0)
        def _():
            up(step, p, z - 1 - step).wait_recv()
            if step < rows - 2:

                @pl.when(z < rows - 1)
                def _():
                    up(step + 1, p, z - 1 - step).start()

            deliver(p, z - 1 - step)

        @pl.when(z + 1 + step < rows)
        def _():
            down(step, p, z + 1 + step).wait_recv()
            if step < rows - 2:

                @pl.when(z > 0)
                def _():
                    down(step + 1, p, z + 1 + step).start()

            deliver(p, z + 1 + step)

        if step == 0:
            for other in range(1, chips):
                pair(p, other).wait_recv()
                pair(p, other).start()

    def multiply(p):
        for owner in range(cols):
            for offset in range(ratio):
                ref = right.at[owner, offset, part(p)]
                pltpu.make_async_copy(ref, ref, swap_recv.at[owner, offset, p]).wait()
        for other in range(chips):
            owner = 2 * lax.rem(x + other, chips) + 1 - core
            left_copy(p, owner, twin, pair_send.at[other, p]).wait_recv()

        def widen(owner, carry):
            left32[pl.ds(owner * piece, piece)] = left[owner, part(p)].astype(F32)
            return carry

        lax.fori_loop(0, cols, widen, 0)
        groups = i_count // GROUP

        def block(at, carry):
            offset, first = at // groups, pl.multiple_of((at % groups) * GROUP, GROUP)
            js = pl.ds(pl.multiple_of(offset * i_count, i_count), i_count)

            def add(owner, sums):
                for k in range(piece):
                    other = right[owner, offset, p * piece + k].astype(F32)
                    sums = tuple(
                        total + left32[owner * piece + k, pl.ds(first + g, 1), :] * other
                        for g, total in enumerate(sums)
                    )
                return sums

            sums = tuple(tri[first + g, js, :] for g in range(GROUP))
            sums = lax.fori_loop(0, cols, add, sums)
            for g in range(GROUP):
                tri[first + g, js, :] = sums[g]
            return carry

        lax.fori_loop(0, groups * ratio, block, 0)

    for step in range(rows - 2):
        for p in range(PIECES):
            relay(step, p)
    for p in range(PIECES):
        relay(rows - 2, p)
        if p > 0:
            multiply(p - 1)
    multiply(PIECES - 1)

    def finish(g, carry):
        span = pl.ds(pl.multiple_of(g * flat, flat), flat)
        values = tri[pl.ds(g * GROUP, GROUP)].reshape(flat, hidden)
        normed = layer_norm(values, out_gain_ref[...], out_bias_ref[...]).astype(BF16)
        out_ref[span, :] = gate[span, :] * jnp.dot(normed, w_out_ref[...], preferred_element_type=F32)
        return carry

    lax.fori_loop(0, i_count // GROUP, finish, 0)

    for p in range(PIECES):
        for step in range(rows - 1):

            @pl.when((z < rows - 1) & (z - step >= 0))
            def _():
                up(step, p, z - step).wait_send()

            @pl.when((z > 0) & (z + step < rows))
            def _():
                down(step, p, z + step).wait_send()

        for step in range(1, chips):
            far(p, step).wait_send()
        for step in range(chips):
            pair(p, step).wait_send()
        for block in range(rows):

            @pl.when(block // ratio != c)
            def _():
                swap(p, block).wait_send()


def solution(mesh):
    rows, cols = mesh.shape["row"], mesh.shape["col"]

    def body(pair_acts, residue_mask, norm_gain, norm_bias, w_left, w_right, w_gate, out_gain, out_bias, w_out):
        i_count, k_count, channels = pair_acts.shape
        hidden = w_out.shape[0]
        ratio = rows // cols
        piece = k_count // PIECES
        dma = pltpu.SemaphoreType.DMA
        vmem = pl.BlockSpec(memory_space=pltpu.VMEM)
        flat = pl.pallas_call(
            functools.partial(kernel, rows, cols),
            out_shape=jax.ShapeDtypeStruct((i_count * k_count, channels), F32),
            in_specs=[pl.BlockSpec(memory_space=pl.ANY)] * 10,
            out_specs=vmem,
            scratch_shapes=[
                pltpu.SMEM(residue_mask.shape, jnp.int32),
                pltpu.VMEM((i_count * k_count, channels), F32),
                pltpu.VMEM((1, channels), F32),
                pltpu.VMEM((1, channels), F32),
                pltpu.VMEM(w_left.shape, BF16),
                pltpu.VMEM(w_right.shape, BF16),
                pltpu.VMEM(w_gate.shape, BF16),
                pltpu.VMEM((1, hidden), F32),
                pltpu.VMEM((1, hidden), F32),
                pltpu.VMEM(w_out.shape, BF16),
                pltpu.VMEM((rows, k_count, i_count, hidden), BF16),
                pltpu.VMEM((cols, ratio, k_count, i_count, hidden), BF16),
                pltpu.VMEM((cols, k_count, i_count, hidden), BF16),
                pltpu.VMEM((cols * piece, i_count, hidden), F32),
                pltpu.VMEM((i_count, k_count, hidden), F32),
                pltpu.VMEM((i_count * k_count, channels), F32),
                pltpu.VMEM((i_count, hidden), F32),
                dma((rows - 1, PIECES)),
                dma((rows - 1, PIECES)),
                dma((rows - 1, PIECES)),
                dma((rows - 1, PIECES)),
                dma((rows, PIECES)),
                dma((cols, ratio, PIECES)),
                dma((cols // 2 - 1, PIECES)),
                dma((cols // 2, PIECES)),
                dma((cols, PIECES)),
                dma((10,)),
            ],
            compiler_params=pltpu.CompilerParams(
                collective_id=0, has_side_effects=True, vmem_limit_bytes=60 * 1024 * 1024
            ),
        )(
            residue_mask,
            pair_acts.reshape(i_count * k_count, channels),
            norm_gain.reshape(1, channels),
            norm_bias.reshape(1, channels),
            w_left,
            w_right,
            w_gate,
            out_gain.reshape(1, hidden),
            out_bias.reshape(1, hidden),
            w_out,
        )
        return flat.reshape(i_count, k_count, channels)

    placed = (P(("parts", "row"), "col", None), P("parts"), P(), P(), P(), P(), P(), P(), P(), P())
    return jax.shard_map(
        body,
        mesh=mesh,
        in_specs=placed,
        out_specs=P(("parts", "row"), "col", None),
        check_vma=False,
    )
```

```python
import functools

import jax
import jax.numpy as jnp
from jax import lax
from jax.experimental import pallas as pl
from jax.experimental.pallas import tpu as pltpu
from jax.sharding import PartitionSpec as P

F32 = jnp.float32
BF16 = jnp.bfloat16
PIECES = 4
GROUP = 8


def layer_norm(values, gain, bias):
    mean = jnp.mean(values, axis=-1, keepdims=True)
    centred = values - mean
    var = jnp.mean(centred * centred, axis=-1, keepdims=True)
    return centred * lax.rsqrt(var + 1e-05) * gain + bias


def sigmoid(values):
    return 0.5 * jnp.tanh(0.5 * values) + 0.5


def kernel(
    rows,
    cols,
    *refs,
):
    sources, (out_ref, gate_ref), held = refs[:9], refs[9:11], refs[11:20]
    (
        mask_ref,
        x_ref,
        gain_ref,
        bias_ref,
        w_left_ref,
        w_right_ref,
        w_gate_ref,
        out_gain_ref,
        out_bias_ref,
    ) = held
    (
        chain,
        right,
        left,
        left32,
        tri,
        gate,
        row_valid,
        up_send,
        up_recv,
        down_send,
        down_recv,
        swap_send,
        swap_recv,
        far_send,
        pair_send,
        left_recv,
        load_sem,
    ) = refs[20:]
    loads = [
        pltpu.make_async_copy(source, target, load_sem.at[at])
        for at, (source, target) in enumerate(zip(sources, held))
    ]
    for at in (1, 0, 5, 2, 3, 4, 6, 7, 8):
        loads[at].start()
    z = lax.axis_index("row")
    c = lax.axis_index("col")
    x, core = c // 2, c % 2
    twin = 2 * x + 1 - core
    chips = cols // 2
    ratio = rows // cols
    k_count, i_count, hidden = chain.shape[1:]
    piece = k_count // PIECES
    j_count = ratio * i_count

    barrier = pltpu.get_barrier_semaphore()

    @pl.when(z > 0)
    def _():
        pl.semaphore_signal(barrier, inc=1, device_id={"row": z - 1}, device_id_type=pl.DeviceIdType.MESH)

    @pl.when(z < rows - 1)
    def _():
        pl.semaphore_signal(barrier, inc=1, device_id={"row": z + 1}, device_id_type=pl.DeviceIdType.MESH)

    for step in range(1, cols):
        pl.semaphore_signal(
            barrier, inc=1, device_id={"col": lax.rem(c + step, cols)}, device_id_type=pl.DeviceIdType.MESH
        )

    def part(p):
        return pl.ds(p * piece, piece)

    def up(step, p, block):
        ref = chain.at[block, part(p)]
        return pltpu.make_async_remote_copy(
            ref, ref, up_send.at[step, p], up_recv.at[step, p], {"row": z + 1}, pl.DeviceIdType.MESH
        )

    def down(step, p, block):
        ref = chain.at[block, part(p)]
        return pltpu.make_async_remote_copy(
            ref, ref, down_send.at[step, p], down_recv.at[step, p], {"row": z - 1}, pl.DeviceIdType.MESH
        )

    def swap(p, block):
        return pltpu.make_async_remote_copy(
            chain.at[block, part(p)],
            right.at[c, block % ratio, part(p)],
            swap_send.at[block, p],
            swap_recv.at[c, block % ratio, p],
            {"col": block // ratio},
            pl.DeviceIdType.MESH,
        )

    def keep(p, block):
        return pltpu.make_async_copy(
            chain.at[block, part(p)], right.at[c, block % ratio, part(p)], swap_recv.at[c, block % ratio, p]
        )

    def deliver(p, block):
        @pl.when(block // ratio != c)
        def _():
            swap(p, block).start()

        @pl.when(block // ratio == c)
        def _():
            keep(p, block).start()

    def left_copy(p, owner, target, send):
        ref = left.at[owner, part(p)]
        return pltpu.make_async_remote_copy(
            ref, ref, send, left_recv.at[owner, p], {"col": target}, pl.DeviceIdType.MESH
        )

    def far(p, step):
        return left_copy(p, c, 2 * lax.rem(x + step, chips) + core, far_send.at[step - 1, p])

    def pair(p, step):
        return left_copy(p, 2 * lax.rem(x + step, chips) + core, twin, pair_send.at[step, p])

    loads[0].wait()
    for i in range(i_count):
        row_valid[pl.ds(i, 1), :] = jnp.full((1, hidden), mask_ref[z * i_count + i].astype(F32))

    def side(normed, weight, mask):
        both = jnp.dot(normed, weight, preferred_element_type=F32)
        act = sigmoid(both[:, hidden:]) * both[:, :hidden] * mask
        return act.astype(BF16).reshape(piece, i_count, hidden)

    for at in (2, 3, 1, 5, 4):
        loads[at].wait()
    gain, bias = gain_ref[...], bias_ref[...]
    for p in range(PIECES):
        values = jnp.concatenate(
            [x_ref[pl.ds(p * piece + k, i_count, stride=k_count), :] for k in range(piece)], axis=0
        )
        mask = jnp.concatenate(
            [row_valid[...] * mask_ref[c * k_count + p * piece + k].astype(F32) for k in range(piece)], axis=0
        )
        normed = layer_norm(values, gain, bias).astype(BF16)
        chain[z, part(p)] = side(normed, w_right_ref[...], mask)
        if p == 0:
            neighbours = cols - 1 + (z > 0).astype(jnp.int32) + (z < rows - 1).astype(jnp.int32)
            pl.semaphore_wait(barrier, neighbours)

        @pl.when(z < rows - 1)
        def _():
            up(0, p, z).start()

        @pl.when(z > 0)
        def _():
            down(0, p, z).start()

        left[c, part(p)] = side(normed, w_left_ref[...], mask)
        for step in range(1, chips):
            far(p, step).start()
        pair(p, 0).start()
        deliver(p, z)

    tri[...] = jnp.zeros_like(tri)
    for at in (6, 7, 8):
        loads[at].wait()
    flat = GROUP * k_count

    def make_gate(g, carry):
        span = pl.ds(pl.multiple_of(g * flat, flat), flat)
        normed = layer_norm(x_ref[span, :], gain, bias).astype(BF16)
        gate[span, :] = sigmoid(jnp.dot(normed, w_gate_ref[...], preferred_element_type=F32))
        return carry

    lax.fori_loop(0, i_count // GROUP, make_gate, 0)
    gate_copy = pltpu.make_async_copy(gate, gate_ref, load_sem.at[0])
    gate_copy.start()

    def relay(step, p):
        @pl.when(z - 1 - step >= 0)
        def _():
            up(step, p, z - 1 - step).wait_recv()
            if step < rows - 2:

                @pl.when(z < rows - 1)
                def _():
                    up(step + 1, p, z - 1 - step).start()

            deliver(p, z - 1 - step)

        @pl.when(z + 1 + step < rows)
        def _():
            down(step, p, z + 1 + step).wait_recv()
            if step < rows - 2:

                @pl.when(z > 0)
                def _():
                    down(step + 1, p, z + 1 + step).start()

            deliver(p, z + 1 + step)

        if step == rows - 2:
            for other in range(1, chips):
                pair(p, other).wait_recv()
                pair(p, other).start()

    def multiply(p):
        for owner in range(cols):
            for offset in range(ratio):
                ref = right.at[owner, offset, part(p)]
                pltpu.make_async_copy(ref, ref, swap_recv.at[owner, offset, p]).wait()
        for other in range(chips):
            owner = 2 * lax.rem(x + other, chips) + 1 - core
            left_copy(p, owner, twin, pair_send.at[other, p]).wait_recv()

        def widen(owner, carry):
            left32[pl.ds(owner * piece, piece)] = left[owner, part(p)].astype(F32)
            return carry

        lax.fori_loop(0, cols, widen, 0)
        groups = i_count // GROUP

        def block(at, carry):
            offset, first = at // groups, pl.multiple_of((at % groups) * GROUP, GROUP)
            js = pl.ds(pl.multiple_of(offset * i_count, i_count), i_count)

            def add(owner, sums):
                for k in range(piece):
                    other = right[owner, offset, p * piece + k].astype(F32)
                    sums = tuple(
                        total + left32[owner * piece + k, pl.ds(first + g, 1), :] * other
                        for g, total in enumerate(sums)
                    )
                return sums

            sums = tuple(tri[first + g, js, :] for g in range(GROUP))
            sums = lax.fori_loop(0, cols, add, sums)
            for g in range(GROUP):
                tri[first + g, js, :] = sums[g]
            return carry

        lax.fori_loop(0, groups * ratio, block, 0)

    for step in range(rows - 2):
        for p in range(PIECES):
            relay(step, p)
    for p in range(PIECES):
        relay(rows - 2, p)
        if p > 0:
            multiply(p - 1)
    multiply(PIECES - 1)

    def finish(g, carry):
        span = pl.ds(pl.multiple_of(g * flat, flat), flat)
        values = tri[pl.ds(g * GROUP, GROUP)].reshape(flat, hidden)
        out_ref[span, :] = layer_norm(values, out_gain_ref[...], out_bias_ref[...]).astype(BF16)
        return carry

    lax.fori_loop(0, i_count // GROUP, finish, 0)
    gate_copy.wait()

    for p in range(PIECES):
        for step in range(rows - 1):

            @pl.when((z < rows - 1) & (z - step >= 0))
            def _():
                up(step, p, z - step).wait_send()

            @pl.when((z > 0) & (z + step < rows))
            def _():
                down(step, p, z + step).wait_send()

        for step in range(1, chips):
            far(p, step).wait_send()
        for step in range(chips):
            pair(p, step).wait_send()
        for block in range(rows):

            @pl.when(block // ratio != c)
            def _():
                swap(p, block).wait_send()


def solution(mesh):
    rows, cols = mesh.shape["row"], mesh.shape["col"]

    def body(pair_acts, residue_mask, norm_gain, norm_bias, w_left, w_right, w_gate, out_gain, out_bias, w_out):
        i_count, k_count, channels = pair_acts.shape
        hidden = w_out.shape[0]
        ratio = rows // cols
        piece = k_count // PIECES
        dma = pltpu.SemaphoreType.DMA
        vmem = pl.BlockSpec(memory_space=pltpu.VMEM)
        tri_norm, gate = pl.pallas_call(
            functools.partial(kernel, rows, cols),
            out_shape=(
                jax.ShapeDtypeStruct((i_count * k_count, hidden), BF16),
                jax.ShapeDtypeStruct((i_count * k_count, channels), F32),
            ),
            in_specs=[pl.BlockSpec(memory_space=pl.ANY)] * 9,
            out_specs=(vmem, pl.BlockSpec(memory_space=pl.ANY)),
            scratch_shapes=[
                pltpu.SMEM(residue_mask.shape, jnp.int32),
                pltpu.VMEM((i_count * k_count, channels), F32),
                pltpu.VMEM((1, channels), F32),
                pltpu.VMEM((1, channels), F32),
                pltpu.VMEM(w_left.shape, BF16),
                pltpu.VMEM(w_right.shape, BF16),
                pltpu.VMEM(w_gate.shape, BF16),
                pltpu.VMEM((1, hidden), F32),
                pltpu.VMEM((1, hidden), F32),
                pltpu.VMEM((rows, k_count, i_count, hidden), BF16),
                pltpu.VMEM((cols, ratio, k_count, i_count, hidden), BF16),
                pltpu.VMEM((cols, k_count, i_count, hidden), BF16),
                pltpu.VMEM((cols * piece, i_count, hidden), F32),
                pltpu.VMEM((i_count, k_count, hidden), F32),
                pltpu.VMEM((i_count * k_count, channels), F32),
                pltpu.VMEM((i_count, hidden), F32),
                dma((rows - 1, PIECES)),
                dma((rows - 1, PIECES)),
                dma((rows - 1, PIECES)),
                dma((rows - 1, PIECES)),
                dma((rows, PIECES)),
                dma((cols, ratio, PIECES)),
                dma((cols // 2 - 1, PIECES)),
                dma((cols // 2, PIECES)),
                dma((cols, PIECES)),
                dma((9,)),
            ],
            compiler_params=pltpu.CompilerParams(
                collective_id=0, has_side_effects=True, vmem_limit_bytes=60 * 1024 * 1024
            ),
        )(
            residue_mask,
            pair_acts.reshape(i_count * k_count, channels),
            norm_gain.reshape(1, channels),
            norm_bias.reshape(1, channels),
            w_left,
            w_right,
            w_gate,
            out_gain.reshape(1, hidden),
            out_bias.reshape(1, hidden),
        )
        flat = gate * jnp.dot(tri_norm, w_out, preferred_element_type=F32)
        return flat.reshape(i_count, k_count, channels)

    placed = (P(("parts", "row"), "col", None), P("parts"), P(), P(), P(), P(), P(), P(), P(), P())
    return jax.shard_map(
        body,
        mesh=mesh,
        in_specs=placed,
        out_specs=P(("parts", "row"), "col", None),
        check_vma=False,
    )
```

```python
import functools

import jax
import jax.numpy as jnp
from jax import lax
from jax.experimental import pallas as pl
from jax.experimental.pallas import tpu as pltpu
from jax.sharding import PartitionSpec as P

F32 = jnp.float32
BF16 = jnp.bfloat16
SHARES = (2, 2, 2, 2)
PIECES = len(SHARES)
GROUP = 8


def layer_norm(values, gain, bias):
    mean = jnp.mean(values, axis=-1, keepdims=True)
    centred = values - mean
    var = jnp.mean(centred * centred, axis=-1, keepdims=True)
    return centred * lax.rsqrt(var + 1e-05) * gain + bias


def sigmoid(values):
    return 0.5 * jnp.tanh(0.5 * values) + 0.5


def kernel(
    rows,
    cols,
    *refs,
):
    sources, (out_ref, gate_ref), held = refs[:9], refs[9:11], refs[11:20]
    (
        mask_ref,
        x_ref,
        gain_ref,
        bias_ref,
        w_left_ref,
        w_right_ref,
        w_gate_ref,
        out_gain_ref,
        out_bias_ref,
    ) = held
    (
        chain,
        right,
        left,
        left32,
        tri,
        gate,
        row_valid,
        up_send,
        up_recv,
        down_send,
        down_recv,
        swap_send,
        swap_recv,
        far_send,
        pair_send,
        left_recv,
        load_sem,
    ) = refs[20:]
    loads = [
        pltpu.make_async_copy(source, target, load_sem.at[at])
        for at, (source, target) in enumerate(zip(sources, held))
    ]
    for at in (1, 0, 5, 2, 3, 4, 6, 7, 8):
        loads[at].start()
    z = lax.axis_index("row")
    c = lax.axis_index("col")
    x, core = c // 2, c % 2
    twin = 2 * x + 1 - core
    chips = cols // 2
    ratio = rows // cols
    k_count, i_count, hidden = chain.shape[1:]
    sizes = [share * k_count // sum(SHARES) for share in SHARES]
    starts = [sum(sizes[:p]) for p in range(PIECES)]

    barrier = pltpu.get_barrier_semaphore()

    @pl.when(z > 0)
    def _():
        pl.semaphore_signal(barrier, inc=1, device_id={"row": z - 1}, device_id_type=pl.DeviceIdType.MESH)

    @pl.when(z < rows - 1)
    def _():
        pl.semaphore_signal(barrier, inc=1, device_id={"row": z + 1}, device_id_type=pl.DeviceIdType.MESH)

    for step in range(1, cols):
        pl.semaphore_signal(
            barrier, inc=1, device_id={"col": lax.rem(c + step, cols)}, device_id_type=pl.DeviceIdType.MESH
        )

    def part(p):
        return pl.ds(starts[p], sizes[p])

    def up(step, p, block):
        ref = chain.at[block, part(p)]
        return pltpu.make_async_remote_copy(
            ref, ref, up_send.at[step, p], up_recv.at[step, p], {"row": z + 1}, pl.DeviceIdType.MESH
        )

    def down(step, p, block):
        ref = chain.at[block, part(p)]
        return pltpu.make_async_remote_copy(
            ref, ref, down_send.at[step, p], down_recv.at[step, p], {"row": z - 1}, pl.DeviceIdType.MESH
        )

    def swap(p, block):
        return pltpu.make_async_remote_copy(
            chain.at[block, part(p)],
            right.at[c, block % ratio, part(p)],
            swap_send.at[block, p],
            swap_recv.at[c, block % ratio, p],
            {"col": block // ratio},
            pl.DeviceIdType.MESH,
        )

    def keep(p, block):
        return pltpu.make_async_copy(
            chain.at[block, part(p)], right.at[c, block % ratio, part(p)], swap_recv.at[c, block % ratio, p]
        )

    def deliver(p, block):
        @pl.when(block // ratio != c)
        def _():
            swap(p, block).start()

        @pl.when(block // ratio == c)
        def _():
            keep(p, block).start()

    def left_copy(p, owner, target, send):
        ref = left.at[owner, part(p)]
        return pltpu.make_async_remote_copy(
            ref, ref, send, left_recv.at[owner, p], {"col": target}, pl.DeviceIdType.MESH
        )

    def far(p, step):
        return left_copy(p, c, 2 * lax.rem(x + step, chips) + core, far_send.at[step - 1, p])

    def pair(p, step):
        return left_copy(p, 2 * lax.rem(x + step, chips) + core, twin, pair_send.at[step, p])

    loads[0].wait()
    for i in range(i_count):
        row_valid[pl.ds(i, 1), :] = jnp.full((1, hidden), mask_ref[z * i_count + i].astype(F32))

    def side(normed, weight, mask):
        both = jnp.dot(normed, weight, preferred_element_type=F32)
        act = sigmoid(both[:, hidden:]) * both[:, :hidden] * mask
        return act.astype(BF16).reshape(-1, i_count, hidden)

    for at in (2, 3, 1, 5, 4):
        loads[at].wait()
    gain, bias = gain_ref[...], bias_ref[...]
    for p in range(PIECES):
        values = jnp.concatenate(
            [x_ref[pl.ds(starts[p] + k, i_count, stride=k_count), :] for k in range(sizes[p])], axis=0
        )
        mask = jnp.concatenate(
            [row_valid[...] * mask_ref[c * k_count + starts[p] + k].astype(F32) for k in range(sizes[p])], axis=0
        )
        normed = layer_norm(values, gain, bias).astype(BF16)
        chain[z, part(p)] = side(normed, w_right_ref[...], mask)
        if p == 0:
            neighbours = cols - 1 + (z > 0).astype(jnp.int32) + (z < rows - 1).astype(jnp.int32)
            pl.semaphore_wait(barrier, neighbours)

        @pl.when(z < rows - 1)
        def _():
            up(0, p, z).start()

        @pl.when(z > 0)
        def _():
            down(0, p, z).start()

        left[c, part(p)] = side(normed, w_left_ref[...], mask)
        for step in range(1, chips):
            far(p, step).start()
        pair(p, 0).start()
        deliver(p, z)

    tri[...] = jnp.zeros_like(tri)
    for at in (6, 7, 8):
        loads[at].wait()
    flat = GROUP * k_count

    def make_gate(g, carry):
        span = pl.ds(pl.multiple_of(g * flat, flat), flat)
        normed = layer_norm(x_ref[span, :], gain, bias).astype(BF16)
        gate_ref[span, :] = sigmoid(jnp.dot(normed, w_gate_ref[...], preferred_element_type=F32))
        return carry

    lax.fori_loop(0, i_count // GROUP, make_gate, 0)

    def relay(step, p):
        def upward():
            up(step, p, z - 1 - step).wait_recv()
            if step < rows - 2:

                @pl.when(z < rows - 1)
                def _():
                    up(step + 1, p, z - 1 - step).start()

            deliver(p, z - 1 - step)

        pl.when((z - 1 - step >= 0) & (2 * z >= rows))(upward)

        @pl.when(z + 1 + step < rows)
        def _():
            down(step, p, z + 1 + step).wait_recv()
            if step < rows - 2:

                @pl.when(z > 0)
                def _():
                    down(step + 1, p, z + 1 + step).start()

            deliver(p, z + 1 + step)

        pl.when((z - 1 - step >= 0) & (2 * z < rows))(upward)

        if step == rows - 2:
            for other in range(1, chips):
                pair(p, other).wait_recv()
                pair(p, other).start()

    def multiply(p):
        for owner in range(cols):
            for offset in range(ratio):
                ref = right.at[owner, offset, part(p)]
                pltpu.make_async_copy(ref, ref, swap_recv.at[owner, offset, p]).wait()
        for other in range(chips):
            owner = 2 * lax.rem(x + other, chips) + 1 - core
            left_copy(p, owner, twin, pair_send.at[other, p]).wait_recv()

        piece = sizes[p]

        def widen(owner, carry):
            left32[pl.ds(owner * piece, piece)] = left[owner, part(p)].astype(F32)
            return carry

        lax.fori_loop(0, cols, widen, 0)
        groups = i_count // GROUP

        def block(at, carry):
            offset, first = at // groups, pl.multiple_of((at % groups) * GROUP, GROUP)
            js = pl.ds(pl.multiple_of(offset * i_count, i_count), i_count)

            def add(owner, sums):
                for k in range(piece):
                    other = right[owner, offset, starts[p] + k].astype(F32)
                    sums = tuple(
                        total + left32[owner * piece + k, pl.ds(first + g, 1), :] * other
                        for g, total in enumerate(sums)
                    )
                return sums

            sums = tuple(tri[first + g, js, :] for g in range(GROUP))
            sums = lax.fori_loop(0, cols, add, sums)
            for g in range(GROUP):
                tri[first + g, js, :] = sums[g]
            return carry

        lax.fori_loop(0, groups * ratio, block, 0)

    for step in range(rows - 2):
        for p in range(PIECES):
            relay(step, p)
    for p in range(PIECES):
        relay(rows - 2, p)
        if p > 0:
            multiply(p - 1)
    multiply(PIECES - 1)

    def finish(g, carry):
        span = pl.ds(pl.multiple_of(g * flat, flat), flat)
        values = tri[pl.ds(g * GROUP, GROUP)].reshape(flat, hidden)
        out_ref[span, :] = layer_norm(values, out_gain_ref[...], out_bias_ref[...]).astype(BF16)
        return carry

    lax.fori_loop(0, i_count // GROUP, finish, 0)

    for p in range(PIECES):
        for step in range(rows - 1):

            @pl.when((z < rows - 1) & (z - step >= 0))
            def _():
                up(step, p, z - step).wait_send()

            @pl.when((z > 0) & (z + step < rows))
            def _():
                down(step, p, z + step).wait_send()

        for step in range(1, chips):
            far(p, step).wait_send()
        for step in range(chips):
            pair(p, step).wait_send()
        for block in range(rows):

            @pl.when(block // ratio != c)
            def _():
                swap(p, block).wait_send()


def solution(mesh):
    rows, cols = mesh.shape["row"], mesh.shape["col"]

    def body(pair_acts, residue_mask, norm_gain, norm_bias, w_left, w_right, w_gate, out_gain, out_bias, w_out):
        i_count, k_count, channels = pair_acts.shape
        hidden = w_out.shape[0]
        ratio = rows // cols
        piece = max(SHARES) * k_count // sum(SHARES)
        dma = pltpu.SemaphoreType.DMA
        vmem = pl.BlockSpec(memory_space=pltpu.VMEM)
        tri_norm, gate = pl.pallas_call(
            functools.partial(kernel, rows, cols),
            out_shape=(
                pltpu.VMEM((i_count * k_count, hidden), BF16),
                pltpu.VMEM((i_count * k_count, channels), F32),
            ),
            in_specs=[pl.BlockSpec(memory_space=pl.ANY)] * 9,
            out_specs=(vmem, vmem),
            scratch_shapes=[
                pltpu.SMEM(residue_mask.shape, jnp.int32),
                pltpu.VMEM((i_count * k_count, channels), F32),
                pltpu.VMEM((1, channels), F32),
                pltpu.VMEM((1, channels), F32),
                pltpu.VMEM(w_left.shape, BF16),
                pltpu.VMEM(w_right.shape, BF16),
                pltpu.VMEM(w_gate.shape, BF16),
                pltpu.VMEM((1, hidden), F32),
                pltpu.VMEM((1, hidden), F32),
                pltpu.VMEM((rows, k_count, i_count, hidden), BF16),
                pltpu.VMEM((cols, ratio, k_count, i_count, hidden), BF16),
                pltpu.VMEM((cols, k_count, i_count, hidden), BF16),
                pltpu.VMEM((cols * piece, i_count, hidden), F32),
                pltpu.VMEM((i_count, k_count, hidden), F32),
                pltpu.VMEM((i_count * k_count, channels), F32),
                pltpu.VMEM((i_count, hidden), F32),
                dma((rows - 1, PIECES)),
                dma((rows - 1, PIECES)),
                dma((rows - 1, PIECES)),
                dma((rows - 1, PIECES)),
                dma((rows, PIECES)),
                dma((cols, ratio, PIECES)),
                dma((cols // 2 - 1, PIECES)),
                dma((cols // 2, PIECES)),
                dma((cols, PIECES)),
                dma((9,)),
            ],
            compiler_params=pltpu.CompilerParams(
                collective_id=0, has_side_effects=True, vmem_limit_bytes=60 * 1024 * 1024
            ),
        )(
            residue_mask,
            pair_acts.reshape(i_count * k_count, channels),
            norm_gain.reshape(1, channels),
            norm_bias.reshape(1, channels),
            w_left,
            w_right,
            w_gate,
            out_gain.reshape(1, hidden),
            out_bias.reshape(1, hidden),
        )
        flat = gate * jnp.dot(tri_norm, w_out, preferred_element_type=F32)
        return flat.reshape(i_count, k_count, channels)

    placed = (P(("parts", "row"), "col", None), P("parts"), P(), P(), P(), P(), P(), P(), P(), P())
    return jax.shard_map(
        body,
        mesh=mesh,
        in_specs=placed,
        out_specs=P(("parts", "row"), "col", None),
        check_vma=False,
    )
```

```python
import functools

import jax
import jax.numpy as jnp
from jax import lax
from jax.experimental import pallas as pl
from jax.experimental.pallas import tpu as pltpu
from jax.sharding import PartitionSpec as P

F32 = jnp.float32
BF16 = jnp.bfloat16
SHARES = (2, 2, 2, 2)
PIECES = len(SHARES)
GROUP = 8


def layer_norm(values, gain, bias):
    mean = jnp.mean(values, axis=-1, keepdims=True)
    centred = values - mean
    var = jnp.mean(centred * centred, axis=-1, keepdims=True)
    return centred * lax.rsqrt(var + 1e-05) * gain + bias


def sigmoid(values):
    return 0.5 * jnp.tanh(0.5 * values) + 0.5


def kernel(
    rows,
    cols,
    *refs,
):
    sources, (out_ref, gate_ref), held = refs[:9], refs[9:11], refs[11:20]
    (
        mask_ref,
        x_ref,
        gain_ref,
        bias_ref,
        w_left_ref,
        w_right_ref,
        w_gate_ref,
        out_gain_ref,
        out_bias_ref,
    ) = held
    (
        chain,
        right,
        left,
        left32,
        tri,
        gate,
        row_valid,
        up_send,
        up_recv,
        down_send,
        down_recv,
        swap_send,
        swap_recv,
        far_send,
        pair_send,
        left_recv,
        load_sem,
    ) = refs[20:]
    loads = [
        pltpu.make_async_copy(source, target, load_sem.at[at])
        for at, (source, target) in enumerate(zip(sources, held))
    ]
    for at in (1, 0, 5, 2, 3, 4, 6, 7, 8):
        loads[at].start()
    z = lax.axis_index("row")
    c = lax.axis_index("col")
    x, core = c // 2, c % 2
    twin = 2 * x + 1 - core
    chips = cols // 2
    ratio = rows // cols
    k_count, i_count, hidden = chain.shape[1:]
    sizes = [share * k_count // sum(SHARES) for share in SHARES]
    starts = [sum(sizes[:p]) for p in range(PIECES)]

    barrier = pltpu.get_barrier_semaphore()

    @pl.when(z > 0)
    def _():
        pl.semaphore_signal(barrier, inc=1, device_id={"row": z - 1}, device_id_type=pl.DeviceIdType.MESH)

    @pl.when(z < rows - 1)
    def _():
        pl.semaphore_signal(barrier, inc=1, device_id={"row": z + 1}, device_id_type=pl.DeviceIdType.MESH)

    for step in range(1, cols):
        pl.semaphore_signal(
            barrier, inc=1, device_id={"col": lax.rem(c + step, cols)}, device_id_type=pl.DeviceIdType.MESH
        )

    def part(p):
        return pl.ds(starts[p], sizes[p])

    def up(step, p, block):
        ref = chain.at[block, part(p)]
        return pltpu.make_async_remote_copy(
            ref, ref, up_send.at[step, p], up_recv.at[step, p], {"row": z + 1}, pl.DeviceIdType.MESH
        )

    def down(step, p, block):
        ref = chain.at[block, part(p)]
        return pltpu.make_async_remote_copy(
            ref, ref, down_send.at[step, p], down_recv.at[step, p], {"row": z - 1}, pl.DeviceIdType.MESH
        )

    def swap(p, block):
        return pltpu.make_async_remote_copy(
            chain.at[block, part(p)],
            right.at[c, block % ratio, part(p)],
            swap_send.at[block, p],
            swap_recv.at[c, block % ratio, p],
            {"col": block // ratio},
            pl.DeviceIdType.MESH,
        )

    def keep(p, block):
        return pltpu.make_async_copy(
            chain.at[block, part(p)], right.at[c, block % ratio, part(p)], swap_recv.at[c, block % ratio, p]
        )

    def deliver(p, block):
        @pl.when(block // ratio != c)
        def _():
            swap(p, block).start()

        @pl.when(block // ratio == c)
        def _():
            keep(p, block).start()

    def left_copy(p, owner, target, send):
        ref = left.at[owner, part(p)]
        return pltpu.make_async_remote_copy(
            ref, ref, send, left_recv.at[owner, p], {"col": target}, pl.DeviceIdType.MESH
        )

    def far(p, step):
        return left_copy(p, c, 2 * lax.rem(x + step, chips) + core, far_send.at[step - 1, p])

    def pair(p, step):
        return left_copy(p, 2 * lax.rem(x + step, chips) + core, twin, pair_send.at[step, p])

    loads[0].wait()
    for i in range(i_count):
        row_valid[pl.ds(i, 1), :] = jnp.full((1, hidden), mask_ref[z * i_count + i].astype(F32))

    def side(normed, weight, mask):
        both = jnp.dot(normed, weight, preferred_element_type=F32)
        act = sigmoid(both[:, hidden:]) * both[:, :hidden] * mask
        return act.astype(BF16).reshape(-1, i_count, hidden)

    for at in (2, 3, 1, 5, 4):
        loads[at].wait()
    gain, bias = gain_ref[...], bias_ref[...]
    for p in range(PIECES):
        values = jnp.concatenate(
            [x_ref[pl.ds(starts[p] + k, i_count, stride=k_count), :] for k in range(sizes[p])], axis=0
        )
        mask = jnp.concatenate(
            [row_valid[...] * mask_ref[c * k_count + starts[p] + k].astype(F32) for k in range(sizes[p])], axis=0
        )
        normed = layer_norm(values, gain, bias).astype(BF16)
        chain[z, part(p)] = side(normed, w_right_ref[...], mask)
        if p == 0:
            neighbours = cols - 1 + (z > 0).astype(jnp.int32) + (z < rows - 1).astype(jnp.int32)
            pl.semaphore_wait(barrier, neighbours)

        @pl.when(z < rows - 1)
        def _():
            up(0, p, z).start()

        @pl.when(z > 0)
        def _():
            down(0, p, z).start()

        left[c, part(p)] = side(normed, w_left_ref[...], mask)
        for step in range(1, chips):
            far(p, step).start()
        pair(p, 0).start()
        deliver(p, z)

    tri[...] = jnp.zeros_like(tri)
    for at in (6, 7, 8):
        loads[at].wait()
    flat = GROUP * k_count

    def make_gate(g, carry):
        span = pl.ds(pl.multiple_of(g * flat, flat), flat)
        normed = layer_norm(x_ref[span, :], gain, bias).astype(BF16)
        gate_ref[span, :] = sigmoid(jnp.dot(normed, w_gate_ref[...], preferred_element_type=F32))
        return carry

    lax.fori_loop(0, i_count // GROUP, make_gate, 0)

    def relay(step, p):
        def upward():
            up(step, p, z - 1 - step).wait_recv()
            if step < rows - 2:

                @pl.when(z < rows - 1)
                def _():
                    up(step + 1, p, z - 1 - step).start()

            deliver(p, z - 1 - step)

        pl.when((z - 1 - step >= 0) & (2 * z >= rows))(upward)

        @pl.when(z + 1 + step < rows)
        def _():
            down(step, p, z + 1 + step).wait_recv()
            if step < rows - 2:

                @pl.when(z > 0)
                def _():
                    down(step + 1, p, z + 1 + step).start()

            deliver(p, z + 1 + step)

        pl.when((z - 1 - step >= 0) & (2 * z < rows))(upward)

        if step == rows - 2:
            for other in range(1, chips):
                pair(p, other).wait_recv()
                pair(p, other).start()

    def multiply(p, others):
        owners = [2 * lax.rem(x + other, chips) + side_core for other in others for side_core in range(2)]
        for owner in owners:
            for offset in range(ratio):
                ref = right.at[owner, offset, part(p)]
                pltpu.make_async_copy(ref, ref, swap_recv.at[owner, offset, p]).wait()
        for other in others:
            owner = 2 * lax.rem(x + other, chips) + 1 - core
            left_copy(p, owner, twin, pair_send.at[other, p]).wait_recv()

        piece = sizes[p]

        def owner_at(at):
            return lax.rem(2 * (x + others[0]) + at, cols)

        def widen(at, carry):
            owner = owner_at(at)
            left32[pl.ds(owner * piece, piece)] = left[owner, part(p)].astype(F32)
            return carry

        lax.fori_loop(0, len(owners), widen, 0)
        groups = i_count // GROUP

        def block(at, carry):
            offset, first = at // groups, pl.multiple_of((at % groups) * GROUP, GROUP)
            js = pl.ds(pl.multiple_of(offset * i_count, i_count), i_count)

            def add(at, sums):
                owner = owner_at(at)
                for k in range(piece):
                    other = right[owner, offset, starts[p] + k].astype(F32)
                    sums = tuple(
                        total + left32[owner * piece + k, pl.ds(first + g, 1), :] * other
                        for g, total in enumerate(sums)
                    )
                return sums

            sums = tuple(tri[first + g, js, :] for g in range(GROUP))
            sums = lax.fori_loop(0, len(owners), add, sums)
            for g in range(GROUP):
                tri[first + g, js, :] = sums[g]
            return carry

        lax.fori_loop(0, groups * ratio, block, 0)

    for step in range(rows - 2):
        for p in range(PIECES):
            relay(step, p)
    for p in range(PIECES):
        relay(rows - 2, p)
        if p > 0:
            multiply(p - 1, range(chips))
    multiply(PIECES - 1, range(1))
    multiply(PIECES - 1, range(1, chips))

    def finish(g, carry):
        span = pl.ds(pl.multiple_of(g * flat, flat), flat)
        values = tri[pl.ds(g * GROUP, GROUP)].reshape(flat, hidden)
        out_ref[span, :] = layer_norm(values, out_gain_ref[...], out_bias_ref[...]).astype(BF16)
        return carry

    lax.fori_loop(0, i_count // GROUP, finish, 0)

    for p in range(PIECES):
        for step in range(rows - 1):

            @pl.when((z < rows - 1) & (z - step >= 0))
            def _():
                up(step, p, z - step).wait_send()

            @pl.when((z > 0) & (z + step < rows))
            def _():
                down(step, p, z + step).wait_send()

        for step in range(1, chips):
            far(p, step).wait_send()
        for step in range(chips):
            pair(p, step).wait_send()
        for block in range(rows):

            @pl.when(block // ratio != c)
            def _():
                swap(p, block).wait_send()


def solution(mesh):
    rows, cols = mesh.shape["row"], mesh.shape["col"]

    def body(pair_acts, residue_mask, norm_gain, norm_bias, w_left, w_right, w_gate, out_gain, out_bias, w_out):
        i_count, k_count, channels = pair_acts.shape
        hidden = w_out.shape[0]
        ratio = rows // cols
        piece = max(SHARES) * k_count // sum(SHARES)
        dma = pltpu.SemaphoreType.DMA
        vmem = pl.BlockSpec(memory_space=pltpu.VMEM)
        tri_norm, gate = pl.pallas_call(
            functools.partial(kernel, rows, cols),
            out_shape=(
                pltpu.VMEM((i_count * k_count, hidden), BF16),
                pltpu.VMEM((i_count * k_count, channels), F32),
            ),
            in_specs=[pl.BlockSpec(memory_space=pl.ANY)] * 9,
            out_specs=(vmem, vmem),
            scratch_shapes=[
                pltpu.SMEM(residue_mask.shape, jnp.int32),
                pltpu.VMEM((i_count * k_count, channels), F32),
                pltpu.VMEM((1, channels), F32),
                pltpu.VMEM((1, channels), F32),
                pltpu.VMEM(w_left.shape, BF16),
                pltpu.VMEM(w_right.shape, BF16),
                pltpu.VMEM(w_gate.shape, BF16),
                pltpu.VMEM((1, hidden), F32),
                pltpu.VMEM((1, hidden), F32),
                pltpu.VMEM((rows, k_count, i_count, hidden), BF16),
                pltpu.VMEM((cols, ratio, k_count, i_count, hidden), BF16),
                pltpu.VMEM((cols, k_count, i_count, hidden), BF16),
                pltpu.VMEM((cols * piece, i_count, hidden), F32),
                pltpu.VMEM((i_count, k_count, hidden), F32),
                pltpu.VMEM((i_count * k_count, channels), F32),
                pltpu.VMEM((i_count, hidden), F32),
                dma((rows - 1, PIECES)),
                dma((rows - 1, PIECES)),
                dma((rows - 1, PIECES)),
                dma((rows - 1, PIECES)),
                dma((rows, PIECES)),
                dma((cols, ratio, PIECES)),
                dma((cols // 2 - 1, PIECES)),
                dma((cols // 2, PIECES)),
                dma((cols, PIECES)),
                dma((9,)),
            ],
            compiler_params=pltpu.CompilerParams(
                collective_id=0, has_side_effects=True, vmem_limit_bytes=60 * 1024 * 1024
            ),
        )(
            residue_mask,
            pair_acts.reshape(i_count * k_count, channels),
            norm_gain.reshape(1, channels),
            norm_bias.reshape(1, channels),
            w_left,
            w_right,
            w_gate,
            out_gain.reshape(1, hidden),
            out_bias.reshape(1, hidden),
        )
        flat = gate * jnp.dot(tri_norm, w_out, preferred_element_type=F32)
        return flat.reshape(i_count, k_count, channels)

    placed = (P(("parts", "row"), "col", None), P("parts"), P(), P(), P(), P(), P(), P(), P(), P())
    return jax.shard_map(
        body,
        mesh=mesh,
        in_specs=placed,
        out_specs=P(("parts", "row"), "col", None),
        check_vma=False,
    )
```
